256 devices in a mesh: dp: 8 (over z_hi, y), expert: 16 (over z_lo, x), head: 2 (over core).
Axes of the slice: x: 4, y: 4, z: 8 (z_hi: 2, z_lo: 4; z = z_hi * 4 + z_lo), core: 2. Of those that a mesh axis runs over, the one named last changes fastest.
Arguments:
- prev_rows: bfloat16 [16384, 5120], P(('dp', 'expert'), 'head'), may hold values from -6 to 6
- current: bfloat16 [16384, 5120], P(('dp', 'expert'), 'head'), may hold values from -6 to 6
- expert_ids: int32 [16384, 6], P(('dp', 'expert')), may hold values from 0 to 15, all different within a row; in each aligned block of 128 rows (0 to 127, 128 to 255, ...) at most 72 rows name the same one
- gate_weights: float32 [16384, 6], P(('dp', 'expert')), may hold values from 0.1 to 1
- w_in: bfloat16 [16, 2, 768, 5120], P('expert', None, 'dp', 'head'), may hold values from -0.078125 to 0.078125
- w_down: bfloat16 [16, 768, 5120], P('expert', 'dp', 'head'), may hold values from -0.21875 to 0.21875
Outputs:
- blended: bfloat16 [16384, 5120], P(('dp', 'expert'), 'head')
The draws below stay inside these ranges and needn't reach their ends.
Inputs may be any that keep to these rules, and one draw needn't show every extreme that they name: `expert_ids`: each row names 6 different experts. Within the rows of one index pair of dp and expert (128 aligned rows) no expert is named by more than 72 rows, a bound that some expert reaches in some of these blocks.
All inputs are finite; a program needn't handle non-finite values.
Results may differ from the reference program's by a relative error of at most 0.0052.
Values may be sent and summed in bfloat16 or wider, within the bound.
No kernel may reach another device: no remote copies, remote signals or barrier semaphores. Data moves between devices by JAX's collectives and lax.ppermute only.
A program may use at most 128 MiB of HBM per device.

```python
import math
import jax
import jax.numpy as jnp
import numpy as np
from jax import lax

D = 5120
FF = 768
TOP = 6
TOK_DEV = 128
EXPERTS = 16
CAP = 72
TOKENS = 16384


def levels(key, extent, cuts, smallest, top_value):
    level, own = 1.0, jax.random.fold_in(key, 6)
    for position, parts in cuts:
        heights = jnp.exp(jax.random.uniform(jax.random.fold_in(own, position), (parts,), jnp.float32, smallest / len(cuts), top_value / len(cuts)))
        level = level * jnp.repeat(heights, extent[position] // parts).reshape([-1 if axis == position else 1 for axis in range(len(extent))])
    return level


def assign_block(own_key, own, number, rows, count, top, most, lean):
    order = jax.random.permutation(own_key, count)
    packed, common = shares(count, rows * top, most, lean, True), shares(count, rows * top, most, lean, False)
    places = jnp.arange(count)

    def named(lengths, turn):
        used = int((lengths > 0).sum())
        fixed = max(1, used // 4)
        passed = fixed + (places - fixed + turn * (used - fixed)) % max(1, count - fixed)
        return jnp.zeros((count,), jnp.int32).at[order[jnp.where(places < fixed, places, passed)]].set(jnp.asarray(lengths, jnp.int32))

    lengths = jnp.where(number % 4 == 0, named(packed, number // 4), named(common, number - number // 4 - 1))
    mixed = jax.random.permutation(jax.random.fold_in(own, 3), count)
    source_of, receiver = mixed[0:count // 2 * 2:2], mixed[1:count // 2 * 2:2]
    slack = jnp.minimum(lengths[source_of] - 1, most - lengths[receiver]) // 2
    slack = jnp.where((source_of == order[0]) | (receiver == order[0]) | (lengths[receiver] == 0), 0, jnp.maximum(slack, 0))
    passed = jax.random.randint(jax.random.fold_in(own, 4), (count // 2,), 0, 1 << 20) % (slack + 1)
    lengths = lengths.at[source_of].add(-passed).at[receiver].add(passed)
    labels = jnp.searchsorted(jnp.cumsum(lengths), jnp.arange(rows * top), side="right").astype(jnp.int32)
    grid = labels.reshape(top, rows).T
    grid = grid[jax.random.permutation(jax.random.fold_in(own, 1), rows)]
    turn = jax.random.randint(jax.random.fold_in(own, 2), (rows, 1), 0, top)
    return jnp.take_along_axis(grid, (jnp.arange(top)[None, :] + turn) % top, axis=1)


def shares(count, total, bound, slope, full):
    portions = [(1 << 20) // math.isqrt(grade ** slope) + 1 for grade in range(1, count + 1)]
    largest = bound if full else min(bound, max(-(-total // count), total * portions[0] // sum(portions)))
    least = 1 if total - largest >= count - 1 else 0
    holding, surplus = [largest] + [least] * (count - 1), total - largest - least * (count - 1)
    while surplus > 0:
        candidates = [i for i in range(1, count) if holding[i] < largest] or [i for i in range(1, count) if holding[i] < bound]
        whole, left = sum([portions[i] for i in candidates]), surplus
        for i in candidates:
            addition = min(bound - holding[i], max(1, left * portions[i] // whole), surplus)
            holding[i] = holding[i] + addition
            surplus = surplus - addition
    return np.array(holding)


def gaussian(stream_key, dims, deviation, most, split=(), held_as=jnp.bfloat16):
    array = deviation * jax.random.normal(stream_key, dims, jnp.float32)
    if split:
        array = array * levels(stream_key, dims, split, -0.22, 0.18)
    return jnp.clip(array, -most, most).astype(held_as)


def setup_inputs(seed: int = 0) -> dict:
    key_of = jax.random.split(jax.random.key(seed), 7)
    prev_rows = gaussian(key_of[0], (TOKENS, D), 1.0, 6.0, ((0, 128), (1, 2)))
    current = gaussian(key_of[1], (TOKENS, D), 1.0, 6.0, ((0, 128), (1, 2)))
    expert_ids_keys = jax.random.split(jax.random.fold_in(key_of[2], 1), TOKENS // TOK_DEV)
    expert_ids_turns = jax.random.permutation(jax.random.fold_in(key_of[2], 3), TOKENS // TOK_DEV)
    expert_ids = jax.vmap(lambda own, number: assign_block(jax.random.fold_in(key_of[2], 2), own, number, TOK_DEV, EXPERTS, TOP, CAP, 2))(expert_ids_keys, expert_ids_turns).reshape((TOKENS, TOP))
    gate_weights = jnp.clip(0.1 + 0.9 * jax.random.uniform(key_of[3], (TOKENS, TOP), jnp.float32) ** levels(key_of[3], (TOKENS, TOP), ((0, 128),), -0.2, 0.2), 0.1, 1.0)
    w_in = gaussian(key_of[4], (EXPERTS, 2, FF, D), D ** -0.5, 0.078125, ((0, 16), (2, 8), (3, 2)))
    w_down = gaussian(key_of[5], (EXPERTS, FF, D), FF ** -0.5, 0.21875, ((0, 16), (1, 8), (2, 2)))
    return {"prev_rows": prev_rows, "current": current, "expert_ids": expert_ids, "gate_weights": gate_weights, "w_in": w_in, "w_down": w_down}


def reference(prev_rows, current, expert_ids, gate_weights, w_in, w_down):
    chosen = expert_ids.reshape(-1).astype(jnp.int32)
    flat_gates = gate_weights.reshape(-1)
    owners = (jnp.arange(chosen.shape[0], dtype=jnp.int32) // TOP).astype(jnp.int32)
    most_rows = CAP * (TOKENS // TOK_DEV)
    positions = jnp.arange(most_rows, dtype=jnp.int32)

    def add_expert(expert_index, running):
        ranking = jnp.argsort((chosen != expert_index).astype(jnp.int32), stable=True)[:most_rows]
        live_count = jnp.sum((chosen == expert_index).astype(jnp.int32))
        active = positions < live_count
        token_rows = owners[ranking]
        picked_rows = prev_rows[token_rows]
        inner = w_in[expert_index]
        gate_part = jnp.dot(picked_rows, inner[0].T, preferred_element_type=jnp.float32)
        up_part = jnp.dot(picked_rows, inner[1].T, preferred_element_type=jnp.float32)
        activated = (jax.nn.silu(gate_part) * up_part).astype(jnp.bfloat16)
        produced = jnp.dot(activated, w_down[expert_index], preferred_element_type=jnp.float32)
        produced = lax.optimization_barrier(produced.astype(jnp.bfloat16)).astype(jnp.float32)
        weight = jnp.where(active, flat_gates[ranking], jnp.float32(0.0))
        return running.at[token_rows].add(produced * weight[:, None])

    running = jnp.zeros((TOKENS, D), jnp.float32)
    running = lax.fori_loop(0, EXPERTS, add_expert, running)
    return (current.astype(jnp.float32) + running).astype(jnp.bfloat16)
```

```python
import jax
import jax.numpy as jnp
from jax import lax
from jax.sharding import PartitionSpec as P

NX, NY, NZ, NLO = 4, 4, 8, 4
CAP = 72
BF = jnp.bfloat16
F32 = jnp.float32
AXES = ("dp", "expert")
XGROUPS = [[NX * i + j for j in range(NX)] for i in range(NLO)]
YGROUPS = [[NY * i + j for j in range(NY)] for i in range(NZ // NLO)]


def place(i):
    dp, ex = divmod(i, NLO * NX)
    zh, y = divmod(dp, NY)
    zl, x = divmod(ex, NX)
    return x, y, zh * NLO + zl


def index(x, y, z):
    z %= NZ
    return ((z // NLO) * NY + y % NY) * NLO * NX + (z % NLO) * NX + x % NX


def shift(v, dy=0, dz=0):
    pairs = []
    for i in range(NX * NY * NZ):
        x, y, z = place(i)
        pairs.append((i, index(x, y + dy, z + dz)))
    return lax.ppermute(v, AXES, pairs)


def skip(v, sign):
    pairs = []
    for i in range(NX * NY * NZ):
        x, y, z = place(i)
        pairs.append((i, index(x, y, z + 2 * sign * (1 if z % 2 == 0 else -1))))
    return lax.ppermute(v, AXES, pairs)


def swap_x(v):
    return lax.all_to_all(
        v, "expert", split_axis=0, concat_axis=0, tiled=True, axis_index_groups=XGROUPS
    )


def after(v, *others):
    return lax.optimization_barrier((v,) + others)[0]


def spread_y(v, axis):
    left = shift(v, dy=1)
    right = shift(v, dy=-1)
    half = v.shape[0] // 2
    far = jnp.concatenate([shift(left[:half], dy=1), shift(right[half:], dy=-1)], axis=0)
    return jnp.concatenate([v, left, right, far], axis=axis)


def route(ids, gates, first):
    count = ids.shape[0]
    experts = first + jnp.arange(NX, dtype=jnp.int32)
    hit = ids[:, None, :] == experts[None, :, None]
    member = jnp.any(hit, axis=2)
    weight = jnp.sum(jnp.where(hit, gates[:, None, :], 0.0), axis=2)
    row = lax.broadcasted_iota(jnp.int32, (count, count), 0)
    col = lax.broadcasted_iota(jnp.int32, (count, count), 1)
    position = jnp.dot((col < row).astype(BF), member.astype(BF), preferred_element_type=F32)
    slots = jnp.arange(CAP, dtype=jnp.int32).astype(F32)
    chosen = member[:, :, None] & (position[:, :, None] == slots[None, None, :])
    high = lax.reduce_precision(weight, 8, 7)
    low = weight - high
    pick = chosen.reshape(count, NX * CAP)
    spread = lambda w: jnp.where(chosen, w[:, :, None], 0.0).astype(BF).reshape(count, NX * CAP)
    return pick.astype(BF).T, spread(high), spread(low)


def local(prev_rows, current, expert_ids, gate_weights, w_in, w_down):
    fanout = expert_ids.shape[1]
    first = (lax.axis_index("expert") // NX) * NX
    w_in, w_down = w_in[0], w_down[0]

    small = jnp.concatenate([expert_ids.astype(F32), gate_weights], axis=1)
    smalls = [small, shift(small, dz=1), shift(small, dz=-1), skip(small, 1)]
    blocks = [prev_rows, shift(prev_rows, dz=1), shift(prev_rows, dz=-1), skip(prev_rows, 1)]
    routes = [route(s[:, :fanout].astype(jnp.int32), s[:, fanout:], first) for s in smalls]

    near_in = lax.all_gather(w_in, "dp", axis=1, tiled=True, axis_index_groups=YGROUPS)
    near_down = lax.all_gather(w_down, "dp", axis=0, tiled=True, axis_index_groups=YGROUPS)
    other_in = shift(after(w_in, blocks[1], blocks[2]), dz=NLO)
    other_down = shift(after(w_down, blocks[3]), dz=NLO)
    far_in = spread_y(other_in, 1)
    far_down = spread_y(other_down, 0)

    sent = [jnp.dot(r[0], b, preferred_element_type=F32).astype(BF) for r, b in zip(routes, blocks)]
    mine = swap_x(sent[0])
    rest = jnp.stack([s.reshape(NX, CAP, -1) for s in sent[1:]], axis=1).reshape(NX, 3 * CAP, -1)
    rest = swap_x(rest)
    rows = jnp.concatenate(
        [mine.reshape(NX, 1, CAP, -1), rest.reshape(NX, 3, CAP, -1)], axis=1
    ).reshape(NX * 4 * CAP, -1)

    def project(weights):
        value = lax.dot_general(
            rows,
            weights.reshape(-1, weights.shape[2]),
            (((1,), (1,)), ((), ())),
            preferred_element_type=F32,
        )
        other = lax.ppermute(value.astype(BF), "head", [(0, 1), (1, 0)])
        total = value + other.astype(F32)
        width = total.shape[1] // 2
        return (jax.nn.silu(total[:, :width]) * total[:, width:]).astype(BF)

    hidden_near = project(near_in).reshape(NX, 4, CAP, -1)
    hidden_far = project(far_in).reshape(NX, 4, CAP, -1)
    hidden = jnp.concatenate([hidden_near, hidden_far], axis=3)
    down = jnp.concatenate([near_down, far_down], axis=0)

    partials = [None] * 4
    for b in (3, 1, 2, 0):
        produced = jnp.dot(
            hidden[:, b].reshape(NX * CAP, -1), down, preferred_element_type=F32
        ).astype(BF)
        returned = swap_x(produced)
        _, high, low = routes[b]
        partials[b] = jnp.dot(high, returned, preferred_element_type=F32) + jnp.dot(
            low, returned, preferred_element_type=F32
        )
    total = current.astype(F32) + partials[0]
    total = total + skip(partials[3].astype(BF), -1).astype(F32)
    total = total + shift(partials[1].astype(BF), dz=-1).astype(F32)
    total = total + shift(partials[2].astype(BF), dz=1).astype(F32)
    return total.astype(BF)


def solution(mesh):
    placed = (
        P(("dp", "expert"), "head"),
        P(("dp", "expert"), "head"),
        P(("dp", "expert"), None),
        P(("dp", "expert"), None),
        P("expert", None, "dp", "head"),
        P("expert", "dp", "head"),
    )
    return jax.shard_map(
        local, mesh=mesh, in_specs=placed, out_specs=P(("dp", "expert"), "head"), check_vma=False
    )
```

```python
import jax
import jax.numpy as jnp
from jax import lax
from jax.sharding import PartitionSpec as P

NX, NY, NZ, NLO = 4, 4, 8, 4
CAP = 72
BF = jnp.bfloat16
F32 = jnp.float32
AXES = ("dp", "expert")
XGROUPS = [[NX * i + j for j in range(NX)] for i in range(NLO)]
YGROUPS = [[NY * i + j for j in range(NY)] for i in range(NZ // NLO)]


def place(i):
    dp, ex = divmod(i, NLO * NX)
    zh, y = divmod(dp, NY)
    zl, x = divmod(ex, NX)
    return x, y, zh * NLO + zl


def index(x, y, z):
    z %= NZ
    return ((z // NLO) * NY + y % NY) * NLO * NX + (z % NLO) * NX + x % NX


def shift(v, dy=0, dz=0):
    pairs = []
    for i in range(NX * NY * NZ):
        x, y, z = place(i)
        pairs.append((i, index(x, y + dy, z + dz)))
    return lax.ppermute(v, AXES, pairs)


def skip(v, sign):
    pairs = []
    for i in range(NX * NY * NZ):
        x, y, z = place(i)
        pairs.append((i, index(x, y, z + 2 * sign * (1 if z % 2 == 0 else -1))))
    return lax.ppermute(v, AXES, pairs)


def swap_x(v):
    return lax.all_to_all(
        v, "expert", split_axis=0, concat_axis=0, tiled=True, axis_index_groups=XGROUPS
    )


def route(small, experts):
    ids, gates = jnp.split(small.astype(F32), 2, axis=2)
    count = small.shape[1]
    hit = ids[:, :, None, :] == experts.astype(F32)[None, None, :, None]
    member = jnp.any(hit, axis=3)
    weight = jnp.sum(jnp.where(hit, gates[:, :, None, :], 0.0), axis=3)
    row = lax.broadcasted_iota(jnp.int32, (count, count), 0)
    col = lax.broadcasted_iota(jnp.int32, (count, count), 1)
    position = jnp.einsum(
        "tu,bue->bte", (col < row).astype(BF), member.astype(BF), preferred_element_type=F32
    )
    slots = jnp.arange(CAP, dtype=jnp.int32).astype(F32)
    chosen = member[..., None] & (position[..., None] == slots)
    return chosen, weight


def local(prev_rows, current, expert_ids, gate_weights, w_in, w_down):
    width = prev_rows.shape[1]
    wide = width // 2
    tokens, fanout = expert_ids.shape
    me = lax.axis_index("expert")
    mine_x, mine_z = me % NX, me // NX
    lane = jnp.arange(NX, dtype=jnp.int32)
    w_in, down = w_in[0], w_down[0]
    ff = down.shape[0]

    small = jnp.concatenate(
        [
            expert_ids.astype(BF),
            gate_weights.astype(BF),
            jnp.zeros((tokens, 128 - 2 * fanout), BF),
        ],
        axis=1,
    )
    ext = jnp.concatenate([prev_rows, small], axis=1)

    blocks = [shift(ext, dz=1), shift(ext, dz=-1), skip(ext, 1)]

    shards = jnp.concatenate([w_in.reshape(4, ff // 2, width), down.reshape(2, ff // 2, width)])
    near = lax.all_gather(shards, "dp", axis=1, tiled=True, axis_index_groups=YGROUPS)
    near_in = near[:4].reshape(-1, width)
    near_down = near[4:].reshape(-1, width)

    ins = [shift(w_in, dz=NLO)]

    first = small[None, :, : 2 * fanout]
    experts = mine_z * NX + lane
    chosen, weight = route(first, experts)
    own_pick = chosen[0].transpose(1, 2, 0).reshape(NX * CAP, tokens).astype(BF)
    own_sent = jnp.dot(own_pick, prev_rows, preferred_element_type=F32).astype(BF)
    small_x = swap_x(jnp.tile(small[None], (NX, 1, 1)))
    own_sent, small_x = lax.optimization_barrier((own_sent, small_x))
    mine = swap_x(own_sent)
    chosen_rest, weight_rest = route(
        jnp.stack([b[:, width:] for b in blocks])[:, :, : 2 * fanout], experts
    )
    same = jnp.eye(3, dtype=jnp.bool_)
    rest_pick = chosen_rest.transpose(2, 0, 3, 1)[:, :, :, None, :] & same[None, :, None, :, None]
    rest_sent = jnp.dot(
        rest_pick.reshape(NX * 3 * CAP, 3 * tokens).astype(BF),
        jnp.concatenate([b[:, :width] for b in blocks], axis=0),
        preferred_element_type=F32,
    ).astype(BF)
    chosen = jnp.concatenate([chosen, chosen_rest])
    weight = jnp.concatenate([weight, weight_rest])

    same = jnp.eye(4, dtype=jnp.bool_)
    mask = chosen[:, :, :, None, :] & same[:, None, None, :, None]
    left_share = jnp.where(mask, weight[:, :, :, None, None], 0.0).astype(BF)
    left_share = left_share.reshape(NX * tokens, -1)

    step = jnp.where(mine_z % 2 == 0, 2, -2)
    sources = jnp.stack([mine_z, mine_z + 1, mine_z - 1, mine_z + step]) % NLO
    small_x = small_x.reshape(NX, tokens, -1)[:, :, : 2 * fanout]
    chosen_x, weight_x = route(small_x, sources * NX + mine_x)
    right_shares = []
    for s in range(4):
        mask = chosen_x[:, :, s, None, :] & same[:, None, :, None]
        share = jnp.where(mask, weight_x[:, :, s, None, None], 0.0).astype(BF)
        right_shares.append(share.reshape(NX * tokens, -1))

    ins[0], down, mine, rest_sent = lax.optimization_barrier((ins[0], down, mine, rest_sent))
    rest = swap_x(rest_sent)
    downs = [shift(down, dz=NLO)]
    ins += [shift(ins[0], dy=1), shift(ins[0], dy=-1), shift(ins[0], dy=2)]
    downs[0], ins, left_share, right_shares = lax.optimization_barrier(
        (downs[0], ins, left_share, right_shares)
    )
    downs += [shift(downs[0], dy=1), shift(downs[0], dy=-1), shift(downs[0], dy=2)]
    far_in = jnp.concatenate(ins, axis=1).reshape(-1, width)

    rows = jnp.concatenate(
        [mine.reshape(NX, 1, CAP, width), rest.reshape(NX, 3, CAP, width)], axis=1
    ).reshape(NX * 4 * CAP, width)

    def project(weights):
        value = lax.dot_general(
            rows, weights, (((1,), (1,)), ((), ())), preferred_element_type=F32
        )
        other = lax.ppermute(value.astype(BF), "head", [(0, 1), (1, 0)])
        total = value + other.astype(F32)
        units = total.shape[1] // 2
        return (jax.nn.silu(total[:, :units]) * total[:, units:]).astype(BF)

    hidden = jnp.concatenate([project(near_in), project(far_in)], axis=1)
    down = jnp.concatenate([near_down] + downs, axis=0)

    swapped = hidden.reshape(NX, 4, CAP, -1).transpose(1, 0, 2, 3).reshape(4 * NX * CAP, -1)
    right = jnp.dot(swapped, down[:, wide:], preferred_element_type=F32).astype(BF)
    right = right.reshape(4, NX * CAP, wide)
    right, hidden = lax.optimization_barrier((right, hidden))
    left = jnp.dot(hidden, down[:, :wide], preferred_element_type=F32).astype(BF)

    backs = [right[0], shift(right[1], dz=-1), shift(right[2], dz=1), skip(right[3], -1)]
    left_back = swap_x(left)

    left_part = jnp.dot(left_share, left_back, preferred_element_type=F32)
    left_part = left_part.reshape(4, tokens, wide)

    right_part = 0.0
    for share, back in zip(right_shares, backs):
        right_part = right_part + jnp.dot(share, back, preferred_element_type=F32)
    right_back = swap_x(right_part.astype(BF)).reshape(NX, tokens, wide)

    left_sum = current[:, :wide].astype(F32) + left_part[0]
    left_sum = left_sum + shift(left_part[1].astype(BF), dz=-1).astype(F32)
    left_sum = left_sum + shift(left_part[2].astype(BF), dz=1).astype(F32)
    left_sum = left_sum + skip(left_part[3].astype(BF), -1).astype(F32)
    right_sum = current[:, wide:].astype(F32) + jnp.sum(right_back.astype(F32), axis=0)
    return jnp.concatenate([left_sum.astype(BF), right_sum.astype(BF)], axis=1)


def solution(mesh):
    placed = (
        P(("dp", "expert"), "head"),
        P(("dp", "expert"), "head"),
        P(("dp", "expert"), None),
        P(("dp", "expert"), None),
        P("expert", None, "dp", "head"),
        P("expert", "dp", "head"),
    )
    return jax.shard_map(
        local, mesh=mesh, in_specs=placed, out_specs=P(("dp", "expert"), "head"), check_vma=False
    )
```

```python
import jax
import jax.numpy as jnp
from jax import lax
from jax.sharding import PartitionSpec as P

NX, NY, NZ, NLO = 4, 4, 8, 4
CAP = 72
BF = jnp.bfloat16
F32 = jnp.float32
AXES = ("dp", "expert")
XGROUPS = [[NX * i + j for j in range(NX)] for i in range(NLO)]
YGROUPS = [[NY * i + j for j in range(NY)] for i in range(NZ // NLO)]


def place(i):
    dp, ex = divmod(i, NLO * NX)
    zh, y = divmod(dp, NY)
    zl, x = divmod(ex, NX)
    return x, y, zh * NLO + zl


def index(x, y, z):
    z %= NZ
    return ((z // NLO) * NY + y % NY) * NLO * NX + (z % NLO) * NX + x % NX


def shift(v, dy=0, dz=0):
    pairs = []
    for i in range(NX * NY * NZ):
        x, y, z = place(i)
        pairs.append((i, index(x, y + dy, z + dz)))
    return lax.ppermute(v, AXES, pairs)


def skip(v, sign):
    pairs = []
    for i in range(NX * NY * NZ):
        x, y, z = place(i)
        pairs.append((i, index(x, y, z + 2 * sign * (1 if z % 2 == 0 else -1))))
    return lax.ppermute(v, AXES, pairs)


def swap_x(v):
    return lax.all_to_all(
        v, "expert", split_axis=0, concat_axis=0, tiled=True, axis_index_groups=XGROUPS
    )


def route(small, experts):
    ids, gates = jnp.split(small.astype(F32), 2, axis=2)
    count = small.shape[1]
    hit = ids[:, :, None, :] == experts.astype(F32)[None, None, :, None]
    member = jnp.any(hit, axis=3)
    weight = jnp.sum(jnp.where(hit, gates[:, :, None, :], 0.0), axis=3)
    row = lax.broadcasted_iota(jnp.int32, (count, count), 0)
    col = lax.broadcasted_iota(jnp.int32, (count, count), 1)
    position = jnp.einsum(
        "tu,bue->bte", (col < row).astype(BF), member.astype(BF), preferred_element_type=F32
    )
    slots = jnp.arange(CAP, dtype=jnp.int32).astype(F32)
    chosen = member[..., None] & (position[..., None] == slots)
    return chosen, weight


def local(prev_rows, current, expert_ids, gate_weights, w_in, w_down):
    width = prev_rows.shape[1]
    wide = width // 2
    tokens, fanout = expert_ids.shape
    me = lax.axis_index("expert")
    mine_x, mine_z = me % NX, me // NX
    lane = jnp.arange(NX, dtype=jnp.int32)
    w_in, down = w_in[0], w_down[0]
    ff = down.shape[0]

    small = jnp.concatenate([expert_ids.astype(BF), gate_weights.astype(BF)], axis=1)
    line = jnp.pad(small.reshape(1, -1), ((0, 7), (0, width - 2 * tokens * fanout)))
    ext = jnp.concatenate([prev_rows, line], axis=0)
    shards = jnp.concatenate([w_in.reshape(4, ff // 2, width), down.reshape(2, ff // 2, width)])
    ext, small, shards = lax.optimization_barrier((ext, small, shards))

    near = lax.all_gather(shards, "dp", axis=1, tiled=True, axis_index_groups=YGROUPS)

    blocks = [shift(ext, dz=1), shift(ext, dz=-1), skip(ext, 1)]

    ins = [shift(w_in, dz=NLO)]

    experts = mine_z * NX + lane
    chosen, weight = route(small[None], experts)
    own_pick = chosen[0].transpose(1, 2, 0).reshape(NX * CAP, tokens).astype(BF)
    own_sent = jnp.dot(own_pick, prev_rows, preferred_element_type=F32).astype(BF)
    small_x = swap_x(jnp.tile(jnp.pad(small, ((0, 0), (0, 128 - 2 * fanout)))[None], (NX, 1, 1)))
    own_sent, small_x = lax.optimization_barrier((own_sent, small_x))
    mine = swap_x(own_sent)
    lines = jnp.stack([b[tokens, : 2 * tokens * fanout] for b in blocks])
    chosen_rest, weight_rest = route(lines.reshape(3, tokens, 2 * fanout), experts)
    same = jnp.eye(3, dtype=jnp.bool_)
    rest_pick = jnp.pad(chosen_rest.transpose(2, 0, 3, 1), ((0, 0), (0, 0), (0, 0), (0, 8)))
    rest_pick = rest_pick[:, :, :, None, :] & same[None, :, None, :, None]
    rest_sent = jnp.dot(
        rest_pick.reshape(NX * 3 * CAP, -1).astype(BF),
        jnp.concatenate(blocks, axis=0),
        preferred_element_type=F32,
    ).astype(BF)
    chosen = jnp.concatenate([chosen, chosen_rest])
    weight = jnp.concatenate([weight, weight_rest])

    same = jnp.eye(4, dtype=jnp.bool_)
    mask = chosen[:, :, :, None, :] & same[:, None, None, :, None]
    left_share = jnp.where(mask, weight[:, :, :, None, None], 0.0).astype(BF)
    left_share = left_share.reshape(NX * tokens, -1)

    step = jnp.where(mine_z % 2 == 0, 2, -2)
    sources = jnp.stack([mine_z, mine_z + 1, mine_z - 1, mine_z + step]) % NLO
    small_x = small_x.reshape(NX, tokens, -1)[:, :, : 2 * fanout]
    chosen_x, weight_x = route(small_x, sources * NX + mine_x)
    right_shares = []
    for s in range(4):
        mask = chosen_x[:, :, s, None, :] & same[:, None, :, None]
        share = jnp.where(mask, weight_x[:, :, s, None, None], 0.0).astype(BF)
        right_shares.append(share.reshape(NX * tokens, -1))

    ins[0], down, mine, rest_sent, right_shares = lax.optimization_barrier(
        (ins[0], down, mine, rest_sent, right_shares)
    )
    rest = swap_x(rest_sent)
    downs = [shift(down, dz=NLO)]
    ins += [shift(ins[0], dy=1), shift(ins[0], dy=-1)]
    downs[0], ins, near = lax.optimization_barrier((downs[0], ins, near))
    near_in = near[:4].reshape(-1, width)
    near_down = near[4:].reshape(-1, width)
    far_in = jnp.concatenate(ins + ins[:1], axis=1)
    downs += [shift(downs[0], dy=1), shift(downs[0], dy=-1)]
    far = [shift(ins[1][:1], dy=1), shift(ins[2][1:], dy=-1)]
    downs, far, far_in, near_in, left_share, rest = lax.optimization_barrier(
        (downs, far, far_in, near_in, left_share, rest)
    )
    downs += [shift(downs[1][: ff // 2], dy=1), shift(downs[2][ff // 2 :], dy=-1)]
    far_in = lax.dynamic_update_slice(far_in, far[0], (0, 3 * ff, 0))
    far_in = lax.dynamic_update_slice(far_in, far[1], (1, 3 * ff, 0)).reshape(-1, width)

    rows = jnp.concatenate(
        [mine.reshape(NX, 1, CAP, width), rest.reshape(NX, 3, CAP, width)], axis=1
    ).reshape(NX * 4 * CAP, width)

    def project(weights):
        value = lax.dot_general(
            rows, weights, (((1,), (1,)), ((), ())), preferred_element_type=F32
        )
        other = lax.ppermute(value.astype(BF), "head", [(0, 1), (1, 0)])
        total = value + other.astype(F32)
        units = total.shape[1] // 2
        return (jax.nn.silu(total[:, :units]) * total[:, units:]).astype(BF)

    hidden = jnp.concatenate([project(near_in), project(far_in)], axis=1)
    down = jnp.concatenate([near_down] + downs, axis=0)

    swapped = hidden.reshape(NX, 4, CAP, -1).transpose(1, 0, 2, 3).reshape(4 * NX * CAP, -1)
    right = jnp.dot(swapped, down[:, wide:], preferred_element_type=F32).astype(BF)
    right = right.reshape(4, NX * CAP, wide)
    right, hidden = lax.optimization_barrier((right, hidden))
    left = jnp.dot(hidden, down[:, :wide], preferred_element_type=F32).astype(BF)

    backs = [right[0], shift(right[1], dz=-1), shift(right[2], dz=1), skip(right[3], -1)]
    left_back = swap_x(left)

    left_part = jnp.dot(left_share, left_back, preferred_element_type=F32)
    left_part = left_part.reshape(4, tokens, wide)

    right_part = 0.0
    for share, back in zip(right_shares, backs):
        right_part = right_part + jnp.dot(share, back, preferred_element_type=F32)
    right_back = swap_x(right_part.astype(BF)).reshape(NX, tokens, wide)

    left_sum = current[:, :wide].astype(F32) + left_part[0]
    left_sum = left_sum + shift(left_part[1].astype(BF), dz=-1).astype(F32)
    left_sum = left_sum + shift(left_part[2].astype(BF), dz=1).astype(F32)
    left_sum = left_sum + skip(left_part[3].astype(BF), -1).astype(F32)
    right_sum = current[:, wide:].astype(F32) + jnp.sum(right_back.astype(F32), axis=0)
    return jnp.concatenate([left_sum.astype(BF), right_sum.astype(BF)], axis=1)


def solution(mesh):
    placed = (
        P(("dp", "expert"), "head"),
        P(("dp", "expert"), "head"),
        P(("dp", "expert"), None),
        P(("dp", "expert"), None),
        P("expert", None, "dp", "head"),
        P("expert", "dp", "head"),
    )
    return jax.shard_map(
        local, mesh=mesh, in_specs=placed, out_specs=P(("dp", "expert"), "head"), check_vma=False
    )
```

```python
import jax
import jax.numpy as jnp
from jax import lax
from jax.sharding import PartitionSpec as P

NX, NY, NZ, NLO = 4, 4, 8, 4
CAP = 72
BF = jnp.bfloat16
F32 = jnp.float32
AXES = ("dp", "expert")
XGROUPS = [[NX * i + j for j in range(NX)] for i in range(NLO)]
YGROUPS = [[NY * i + j for j in range(NY)] for i in range(NZ // NLO)]


def place(i):
    dp, ex = divmod(i, NLO * NX)
    zh, y = divmod(dp, NY)
    zl, x = divmod(ex, NX)
    return x, y, zh * NLO + zl


def index(x, y, z):
    z %= NZ
    return ((z // NLO) * NY + y % NY) * NLO * NX + (z % NLO) * NX + x % NX


def shift(v, dy=0, dz=0):
    pairs = []
    for i in range(NX * NY * NZ):
        x, y, z = place(i)
        pairs.append((i, index(x, y + dy, z + dz)))
    return lax.ppermute(v, AXES, pairs)


def skip(v, sign):
    pairs = []
    for i in range(NX * NY * NZ):
        x, y, z = place(i)
        pairs.append((i, index(x, y, z + 2 * sign * (1 if z % 2 == 0 else -1))))
    return lax.ppermute(v, AXES, pairs)


def swap_x(v):
    return lax.all_to_all(
        v, "expert", split_axis=0, concat_axis=0, tiled=True, axis_index_groups=XGROUPS
    )


def route(small, experts):
    ids, gates = jnp.split(small.astype(F32), 2, axis=2)
    count = small.shape[1]
    hit = ids[:, :, None, :] == experts.astype(F32)[None, None, :, None]
    member = jnp.any(hit, axis=3)
    weight = jnp.sum(jnp.where(hit, gates[:, :, None, :], 0.0), axis=3)
    row = lax.broadcasted_iota(jnp.int32, (count, count), 0)
    col = lax.broadcasted_iota(jnp.int32, (count, count), 1)
    position = jnp.einsum(
        "tu,bue->bte", (col < row).astype(BF), member.astype(BF), preferred_element_type=F32
    )
    slots = jnp.arange(CAP, dtype=jnp.int32).astype(F32)
    chosen = member[..., None] & (position[..., None] == slots)
    return chosen, weight


def local(prev_rows, current, expert_ids, gate_weights, w_in, w_down):
    width = prev_rows.shape[1]
    wide = width // 2
    tokens, fanout = expert_ids.shape
    me = lax.axis_index("expert")
    mine_x, mine_z = me % NX, me // NX
    lane = jnp.arange(NX, dtype=jnp.int32)
    w_in, down = w_in[0], w_down[0]
    ff = down.shape[0]

    small = jnp.concatenate([expert_ids.astype(BF), gate_weights.astype(BF)], axis=1)
    line = jnp.pad(small.reshape(1, -1), ((0, 7), (0, width - 2 * tokens * fanout)))
    ext = jnp.concatenate([prev_rows, line], axis=0)
    shards = jnp.concatenate([w_in.reshape(4, ff // 2, width), down.reshape(2, ff // 2, width)])
    ext, small = lax.optimization_barrier((ext, small))

    near = lax.all_gather(shards, "dp", axis=1, tiled=True, axis_index_groups=YGROUPS)

    blocks = [shift(ext, dz=1), shift(ext, dz=-1), skip(ext, 1)]

    experts = mine_z * NX + lane
    chosen, weight = route(small[None], experts)
    own_pick = chosen[0].transpose(1, 2, 0).reshape(NX * CAP, tokens).astype(BF)
    own_sent = jnp.dot(own_pick, prev_rows, preferred_element_type=F32).astype(BF)
    mine = swap_x(own_sent)

    later, blocks, small_x, mine = lax.optimization_barrier((w_in, blocks, small, mine))
    other_in = shift(later, dz=NLO)
    small_x = jnp.pad(small_x, ((0, 0), (0, 128 - 2 * fanout)))
    small_x = swap_x(jnp.tile(small_x[None], (NX, 1, 1)))
    small_x, blocks = lax.optimization_barrier((small_x, blocks))
    lines = jnp.stack([b[tokens, : 2 * tokens * fanout] for b in blocks])
    chosen_rest, weight_rest = route(lines.reshape(3, tokens, 2 * fanout), experts)
    same = jnp.eye(3, dtype=jnp.bool_)
    rest_pick = jnp.pad(chosen_rest.transpose(2, 0, 3, 1), ((0, 0), (0, 0), (0, 0), (0, 8)))
    rest_pick = rest_pick[:, :, :, None, :] & same[None, :, None, :, None]
    rest_sent = jnp.dot(
        rest_pick.reshape(NX * 3 * CAP, -1).astype(BF),
        jnp.concatenate(blocks, axis=0),
        preferred_element_type=F32,
    ).astype(BF)
    chosen = jnp.concatenate([chosen, chosen_rest])
    weight = jnp.concatenate([weight, weight_rest])

    same = jnp.eye(4, dtype=jnp.bool_)
    mask = chosen[:, :, :, None, :] & same[:, None, None, :, None]
    left_share = jnp.where(mask, weight[:, :, :, None, None], 0.0).astype(BF)
    left_share = left_share.reshape(NX * tokens, -1)

    step = jnp.where(mine_z % 2 == 0, 2, -2)
    sources = jnp.stack([mine_z, mine_z + 1, mine_z - 1, mine_z + step]) % NLO
    small_x = small_x.reshape(NX, tokens, -1)[:, :, : 2 * fanout]
    chosen_x, weight_x = route(small_x, sources * NX + mine_x)
    right_shares = []
    for s in range(4):
        mask = chosen_x[:, :, s, None, :] & same[:, None, :, None]
        share = jnp.where(mask, weight_x[:, :, s, None, None], 0.0).astype(BF)
        right_shares.append(share.reshape(NX * tokens, -1))

    rest = swap_x(rest_sent)
    other_in, down, mine = lax.optimization_barrier((other_in, down, mine))
    gates, ups = [other_in[0]], [other_in[1]]
    downs = [shift(down, dz=NLO)]
    gates += [shift(gates[0], dy=1), shift(gates[0], dy=-1)]
    ups += [shift(ups[0], dy=1), shift(ups[0], dy=-1)]
    downs, gates, ups, near = lax.optimization_barrier((downs, gates, ups, near))
    near_in = near[:4].reshape(-1, width)
    near_down = near[4:].reshape(-1, width)
    def added(pair):
        return pair[0].astype(F32) + pair[1].astype(F32)

    far_gate = jnp.concatenate(gates + gates[:1])
    far_up = jnp.concatenate(ups + ups[:1])
    downs += [shift(downs[0], dy=1), shift(downs[0], dy=-1)]
    far = [shift(gates[1], dy=1), shift(ups[2], dy=-1)]
    rows = jnp.concatenate(
        [mine.reshape(NX, 1, CAP, width), rest.reshape(NX, 3, CAP, width)], axis=1
    ).reshape(NX * 4 * CAP, width)
    downs, far, far_gate, far_up, near_in, rows, left_share, right_shares = (
        lax.optimization_barrier(
            (downs, far, far_gate, far_up, near_in, rows, left_share, right_shares)
        )
    )
    def meet(weights):
        value = lax.dot_general(
            rows, weights, (((1,), (1,)), ((), ())), preferred_element_type=F32
        ).astype(BF)
        return value, lax.ppermute(value, "head", [(0, 1), (1, 0)])

    near_both = meet(near_in)
    downs += [shift(downs[1][: ff // 2], dy=1), shift(downs[2][ff // 2 :], dy=-1)]
    far_gate = added(meet(lax.dynamic_update_slice(far_gate, far[0], (3 * ff, 0))))
    far_up = added(meet(lax.dynamic_update_slice(far_up, far[1], (3 * ff, 0))))
    near_both = added(near_both)
    half = NY * ff
    near_hidden = (jax.nn.silu(near_both[:, :half]) * near_both[:, half:]).astype(BF)
    far_hidden = (jax.nn.silu(far_gate) * far_up).astype(BF)
    hidden = jnp.concatenate([near_hidden, far_hidden], axis=1)
    down = jnp.concatenate([near_down] + downs, axis=0)

    swapped = hidden.reshape(NX, 4, CAP, -1).transpose(1, 0, 2, 3).reshape(4 * NX * CAP, -1)
    right = jnp.dot(swapped, down[:, wide:], preferred_element_type=F32).astype(BF)
    right = right.reshape(4, NX * CAP, wide)
    right, hidden = lax.optimization_barrier((right, hidden))
    left = jnp.dot(hidden, down[:, :wide], preferred_element_type=F32).astype(BF)

    backs = [right[0], shift(right[1], dz=-1), shift(right[2], dz=1)]
    last, backs = lax.optimization_barrier((right[3], backs))
    backs.append(skip(last, -1))
    left_back = swap_x(left)

    left_part = jnp.dot(left_share, left_back, preferred_element_type=F32)
    left_part = left_part.reshape(4, tokens, wide)

    right_part = 0.0
    for share, back in zip(right_shares, backs):
        right_part = right_part + jnp.dot(share, back, preferred_element_type=F32)
    right_back = swap_x(right_part.astype(BF)).reshape(NX, tokens, wide)

    left_sum = current[:, :wide].astype(F32) + left_part[0]
    left_sum = left_sum + shift(left_part[1].astype(BF), dz=-1).astype(F32)
    left_sum = left_sum + shift(left_part[2].astype(BF), dz=1).astype(F32)
    left_sum = left_sum + skip(left_part[3].astype(BF), -1).astype(F32)
    right_sum = current[:, wide:].astype(F32) + jnp.sum(right_back.astype(F32), axis=0)
    return jnp.concatenate([left_sum.astype(BF), right_sum.astype(BF)], axis=1)


def solution(mesh):
    placed = (
        P(("dp", "expert"), "head"),
        P(("dp", "expert"), "head"),
        P(("dp", "expert"), None),
        P(("dp", "expert"), None),
        P("expert", None, "dp", "head"),
        P("expert", "dp", "head"),
    )
    return jax.shard_map(
        local, mesh=mesh, in_specs=placed, out_specs=P(("dp", "expert"), "head"), check_vma=False
    )
```

```python
import jax
import jax.numpy as jnp
from jax import lax
from jax.sharding import PartitionSpec as P

NX, NY, NZ, NLO = 4, 4, 8, 4
CAP = 72
BF = jnp.bfloat16
F32 = jnp.float32
AXES = ("dp", "expert")
XGROUPS = [[NX * i + j for j in range(NX)] for i in range(NLO)]
YGROUPS = [[NY * i + j for j in range(NY)] for i in range(NZ // NLO)]


def place(i):
    dp, ex = divmod(i, NLO * NX)
    zh, y = divmod(dp, NY)
    zl, x = divmod(ex, NX)
    return x, y, zh * NLO + zl


def index(x, y, z):
    z %= NZ
    return ((z // NLO) * NY + y % NY) * NLO * NX + (z % NLO) * NX + x % NX


def shift(v, dy=0, dz=0):
    pairs = []
    for i in range(NX * NY * NZ):
        x, y, z = place(i)
        pairs.append((i, index(x, y + dy, z + dz)))
    return lax.ppermute(v, AXES, pairs)


def skip(v, sign):
    pairs = []
    for i in range(NX * NY * NZ):
        x, y, z = place(i)
        pairs.append((i, index(x, y, z + 2 * sign * (1 if z % 2 == 0 else -1))))
    return lax.ppermute(v, AXES, pairs)


def swap_x(v):
    return lax.all_to_all(
        v, "expert", split_axis=0, concat_axis=0, tiled=True, axis_index_groups=XGROUPS
    )


def route(small, experts):
    ids, gates = jnp.split(small.astype(F32), 2, axis=2)
    count = small.shape[1]
    hit = ids[:, :, None, :] == experts.astype(F32)[None, None, :, None]
    member = jnp.any(hit, axis=3)
    weight = jnp.sum(jnp.where(hit, gates[:, :, None, :], 0.0), axis=3)
    row = lax.broadcasted_iota(jnp.int32, (count, count), 0)
    col = lax.broadcasted_iota(jnp.int32, (count, count), 1)
    position = jnp.einsum(
        "tu,bue->bte", (col < row).astype(BF), member.astype(BF), preferred_element_type=F32
    )
    slots = jnp.arange(CAP, dtype=jnp.int32).astype(F32)
    chosen = member[..., None] & (position[..., None] == slots)
    return chosen, weight


def local(prev_rows, current, expert_ids, gate_weights, w_in, w_down):
    width = prev_rows.shape[1]
    wide = width // 2
    tokens, fanout = expert_ids.shape
    me = lax.axis_index("expert")
    mine_x, mine_z = me % NX, me // NX
    lane = jnp.arange(NX, dtype=jnp.int32)
    w_in, down = w_in[0], w_down[0]
    ff = down.shape[0]

    small = jnp.concatenate([expert_ids.astype(BF), gate_weights.astype(BF)], axis=1)
    line = jnp.pad(small.reshape(1, -1), ((0, 7), (0, width - 2 * tokens * fanout)))
    ext = jnp.concatenate([prev_rows, line], axis=0)
    shards = jnp.concatenate([w_in.reshape(4, ff // 2, width), down.reshape(2, ff // 2, width)])
    ext, small = lax.optimization_barrier((ext, small))

    near = lax.all_gather(shards, "dp", axis=1, tiled=True, axis_index_groups=YGROUPS)

    blocks = [shift(ext, dz=1), shift(ext, dz=-1), skip(ext, 1)]

    experts = mine_z * NX + lane
    chosen, weight = route(small[None], experts)
    own_pick = chosen[0].transpose(1, 2, 0).reshape(NX * CAP, tokens).astype(BF)
    own_sent = jnp.dot(own_pick, prev_rows, preferred_element_type=F32).astype(BF)
    mine = swap_x(own_sent)

    later, blocks, small_x, mine = lax.optimization_barrier((w_in, blocks, small, mine))
    other_in = shift(later, dz=NLO)
    small_x = jnp.pad(small_x, ((0, 0), (0, 128 - 2 * fanout)))
    small_x = swap_x(jnp.tile(small_x[None], (NX, 1, 1)))
    lines = jnp.stack([b[tokens, : 2 * tokens * fanout] for b in blocks])
    small_x, blocks = lax.optimization_barrier((small_x, blocks))
    chosen_rest, weight_rest = route(lines.reshape(3, tokens, 2 * fanout), experts)
    same = jnp.eye(3, dtype=jnp.bool_)
    rest_pick = jnp.pad(chosen_rest.transpose(2, 0, 3, 1), ((0, 0), (0, 0), (0, 0), (0, 8)))
    rest_pick = rest_pick[:, :, :, None, :] & same[None, :, None, :, None]
    rest_sent = jnp.dot(
        rest_pick.reshape(NX * 3 * CAP, -1).astype(BF),
        jnp.concatenate(blocks, axis=0),
        preferred_element_type=F32,
    ).astype(BF)
    chosen = jnp.concatenate([chosen, chosen_rest])
    weight = jnp.concatenate([weight, weight_rest])

    same = jnp.eye(4, dtype=jnp.bool_)
    mask = chosen[:, :, :, None, :] & same[:, None, None, :, None]
    left_share = jnp.where(mask, weight[:, :, :, None, None], 0.0).astype(BF)
    left_share = left_share.reshape(NX * tokens, -1)

    step = jnp.where(mine_z % 2 == 0, 2, -2)
    sources = jnp.stack([mine_z, mine_z + 1, mine_z - 1, mine_z + step]) % NLO
    small_x = small_x.reshape(NX, tokens, -1)[:, :, : 2 * fanout]
    chosen_x, weight_x = route(small_x, sources * NX + mine_x)
    right_shares = []
    for s in range(4):
        mask = chosen_x[:, :, s, None, :] & same[:, None, :, None]
        share = jnp.where(mask, weight_x[:, :, s, None, None], 0.0).astype(BF)
        right_shares.append(share.reshape(NX * tokens, -1))

    rest = swap_x(rest_sent)
    other_in, down, mine = lax.optimization_barrier((other_in, down, mine))
    gates, ups = [other_in[0]], [other_in[1]]
    downs = [shift(down, dz=NLO)]
    gates += [shift(gates[0], dy=1), shift(gates[0], dy=-1)]
    ups += [shift(ups[0], dy=1), shift(ups[0], dy=-1)]
    downs, gates, ups, near = lax.optimization_barrier((downs, gates, ups, near))
    near_in = near[:4].reshape(-1, width)
    near_down = near[4:].reshape(-1, width)
    def added(pair):
        return pair[0].astype(F32) + pair[1].astype(F32)

    far_gate = jnp.concatenate(gates + gates[:1])
    far_up = jnp.concatenate(ups + ups[:1])
    downs += [shift(downs[0], dy=1), shift(downs[0], dy=-1)]
    far = [shift(gates[1], dy=1), shift(ups[2], dy=-1)]
    rows = jnp.concatenate(
        [mine.reshape(NX, 1, CAP, width), rest.reshape(NX, 3, CAP, width)], axis=1
    ).reshape(NX * 4 * CAP, width)
    downs, far, far_gate, far_up, near_in, rows, left_share, right_shares = (
        lax.optimization_barrier(
            (downs, far, far_gate, far_up, near_in, rows, left_share, right_shares)
        )
    )
    def meet(weights):
        value = lax.dot_general(
            rows, weights, (((1,), (1,)), ((), ())), preferred_element_type=F32
        ).astype(BF)
        return value, lax.ppermute(value, "head", [(0, 1), (1, 0)])

    near_both = meet(near_in)
    downs += [shift(downs[1][: ff // 2], dy=1), shift(downs[2][ff // 2 :], dy=-1)]
    far_gate = added(meet(lax.dynamic_update_slice(far_gate, far[0], (3 * ff, 0))))
    far_up = added(meet(lax.dynamic_update_slice(far_up, far[1], (3 * ff, 0))))
    near_both = added(near_both)
    half = NY * ff
    near_hidden = (jax.nn.silu(near_both[:, :half]) * near_both[:, half:]).astype(BF)
    far_hidden = (jax.nn.silu(far_gate) * far_up).astype(BF)
    hidden = jnp.concatenate([near_hidden, far_hidden], axis=1)
    down = jnp.concatenate([near_down] + downs, axis=0)

    swapped = hidden.reshape(NX, 4, CAP, -1).transpose(1, 0, 2, 3).reshape(4 * NX * CAP, -1)
    right = jnp.dot(swapped, down[:, wide:], preferred_element_type=F32).astype(BF)
    right = right.reshape(4, NX * CAP, wide)
    right, hidden = lax.optimization_barrier((right, hidden))
    left = jnp.dot(hidden, down[:, :wide], preferred_element_type=F32).astype(BF)

    backs = [right[0], shift(right[1], dz=-1), shift(right[2], dz=1)]
    last, backs = lax.optimization_barrier((right[3], backs))
    backs.append(skip(last, -1))
    left_back = swap_x(left)

    left_part = jnp.dot(left_share, left_back, preferred_element_type=F32)
    left_part = left_part.reshape(4, tokens, wide)

    right_part = 0.0
    for share, back in zip(right_shares, backs):
        right_part = right_part + jnp.dot(share, back, preferred_element_type=F32)
    right_back = swap_x(right_part.astype(BF)).reshape(NX, tokens, wide)

    left_sum = current[:, :wide].astype(F32) + left_part[0]
    left_sum = left_sum + shift(left_part[1].astype(BF), dz=-1).astype(F32)
    left_sum = left_sum + shift(left_part[2].astype(BF), dz=1).astype(F32)
    left_sum = left_sum + skip(left_part[3].astype(BF), -1).astype(F32)
    right_sum = current[:, wide:].astype(F32) + jnp.sum(right_back.astype(F32), axis=0)
    return jnp.concatenate([left_sum.astype(BF), right_sum.astype(BF)], axis=1)


def solution(mesh):
    placed = (
        P(("dp", "expert"), "head"),
        P(("dp", "expert"), "head"),
        P(("dp", "expert"), None),
        P(("dp", "expert"), None),
        P("expert", None, "dp", "head"),
        P("expert", "dp", "head"),
    )
    return jax.shard_map(
        local, mesh=mesh, in_specs=placed, out_specs=P(("dp", "expert"), "head"), check_vma=False
    )
```
